32 devices in a mesh: rows: 4 (over y, x), cols: 4 (over z), depth: 2 (over core).
Axes of the slice: x: 2, y: 2, z: 4, core: 2. Of those that a mesh axis runs over, the one named last changes fastest.
Arguments:
- tile_left: float32 [4, 4, 64, 2048], P('rows', 'cols'), may hold values from -6 to 6
- tile_right: float32 [4, 4, 64, 2048], P('rows', 'cols'), may hold values from -0.75 to 0.75
- left_u: bfloat16 [2, 16, 4, 64, 2048], P('depth', 'cols', 'rows'), may hold values from -6 to 6
- left_v: bfloat16 [2, 16, 4, 64, 2048], P('depth', 'cols', 'rows'), may hold values from -0.0625 to 0.0625
- rank_left: int32 [2, 16, 4], P('depth', 'cols', 'rows'), may hold values from 16 to 64
- right_u: bfloat16 [2, 16, 4, 64, 2048], P('depth', 'rows', 'cols'), may hold values from -6 to 6
- right_v: bfloat16 [2, 16, 4, 64, 2048], P('depth', 'rows', 'cols'), may hold values from -0.0625 to 0.0625
- rank_right: int32 [2, 16, 4], P('depth', 'rows', 'cols'), may hold values from 16 to 64
- triples: int32 [4, 4, 2, 6], P('rows', 'cols', 'depth'), may hold values from -1 to 15, as said below
Outputs:
- new_left: float32 [4, 4, 64, 2048], P('rows', 'cols', None, 'depth')
- new_right: float32 [4, 4, 64, 2048], P('rows', 'cols', None, 'depth')
The draws below stay inside these ranges and needn't reach their ends.
Inputs may be any that keep to these rules, and one draw needn't show every extreme that they name: `triples`: for each tile and layer the first entries are distinct panel numbers of 0 to 15 and the remaining entries are -1; every list has at least one panel number, and in every draw some tile in some layer lists all 6.
All inputs are finite; a program needn't handle non-finite values.
Results may differ from the reference program's by a relative error of at most 0.0043.
Values may be sent and summed in bfloat16 or wider, within the bound.
A program may use at most 128 MiB of HBM per device.

```python
import math
import jax
import jax.numpy as jnp
from jax import lax

NB = 2048
RK = 64
KL = 16
MAXA = 6
NTR = 4
NTC = 4
LAYERS = 2
N_DEPTH = 2


def draw_triples(key, part):
    keys = jax.random.split(jax.random.fold_in(key, 7), 4)
    total = NTR * NTC * LAYERS
    scores = jax.random.randint(keys[0], (total, KL), 0, 1 << 20) * KL + jnp.arange(KL, dtype=jnp.int32)[None, :]
    order = jnp.argsort(scores, axis=1).astype(jnp.int32)[:, :MAXA]
    first = jax.random.randint(keys[1], (total,), 0, MAXA)
    second = jax.random.randint(keys[2], (total,), 0, MAXA)
    counts = 1 + first * second // max(MAXA - 1, 1)
    spot = jax.random.randint(keys[3], (), 0, total)
    counts = jnp.where(jnp.arange(total) == spot, MAXA, counts)
    slots = jnp.arange(MAXA, dtype=jnp.int32)[None, :]
    listed = jnp.where(slots < counts[:, None], order, -1)
    return listed.astype(jnp.int32).reshape(NTR, NTC, LAYERS, MAXA)


def set_ends(result, key, least, top_value):
    longest = result.shape.index(max(result.shape))
    spots = []
    for shift in (0, 1):
        where = [jax.random.randint(jax.random.fold_in(key, axis), (), 0, length) for axis, length in enumerate(result.shape)]
        where[longest] = (where[longest] + shift) % result.shape[longest]
        spots.append(tuple(where))
    return result.at[spots[0]].set(least).at[spots[1]].set(top_value)


def block_scale(stream_key, shape, pieces, least, high):
    factor_of = 1.0
    for position, blocks in pieces:
        heights = jax.random.uniform(jax.random.fold_in(jax.random.fold_in(stream_key, 6), position), (blocks,), jnp.float32, least / len(pieces), high / len(pieces))
        factor_of = factor_of * jnp.repeat(jnp.exp(heights), shape[position] // blocks).reshape((-1,) + (1,) * (len(shape) - 1 - position))
    return factor_of


def bell_draw(stream_key, shape, deviation, reach, cuts=(), kind=jnp.bfloat16):
    array = jax.random.normal(stream_key, shape, jnp.float32) * deviation
    if len(cuts) > 0:
        array = block_scale(stream_key, shape, cuts, -0.22, 0.18) * array
    return jnp.clip(array, min=-reach, max=reach).astype(kind)


def setup_inputs(seed: int = 0) -> dict:
    arg_keys = jax.random.split(jax.random.key(seed), 10)
    tile_left = bell_draw(arg_keys[0], (NTR, NTC, RK, NB), 1.0, 6.0, ((0, 4), (1, 4)), jnp.float32)
    tile_right = bell_draw(arg_keys[1], (NTR, NTC, RK, NB), 0.125, 0.75, ((0, 4), (1, 4)), jnp.float32)
    left_u = bell_draw(arg_keys[2], (LAYERS, KL, NTR, RK, NB), 1.0, 6.0, ((0, 2), (1, 4), (2, 4)))
    left_v = bell_draw(arg_keys[3], (LAYERS, KL, NTR, RK, NB), (NB * RK // 16) ** -0.5, 0.0625, ((0, 2), (1, 4), (2, 4)))
    rank_left = set_ends(jax.random.randint(arg_keys[4], (LAYERS, KL, NTR), RK // 4, RK + 1), jax.random.fold_in(arg_keys[4], 1), RK // 4, RK).astype(jnp.int32)
    right_u = bell_draw(arg_keys[5], (LAYERS, KL, NTC, RK, NB), 1.0, 6.0, ((0, 2), (1, 4), (2, 4)))
    right_v = bell_draw(arg_keys[6], (LAYERS, KL, NTC, RK, NB), (NB * RK // 16) ** -0.5, 0.0625, ((0, 2), (1, 4), (2, 4)))
    rank_right = set_ends(jax.random.randint(arg_keys[7], (LAYERS, KL, NTC), RK // 4, RK + 1), jax.random.fold_in(arg_keys[7], 1), RK // 4, RK).astype(jnp.int32)
    triples = draw_triples(jax.random.fold_in(arg_keys[9], 71), 0)
    return {"tile_left": tile_left, "tile_right": tile_right, "left_u": left_u, "left_v": left_v, "rank_left": rank_left, "right_u": right_u, "right_v": right_v, "rank_right": rank_right, "triples": triples}


HIGHEST = lax.Precision.HIGHEST

def cross(first, second, dim_first, dim_second):
    return lax.dot_general(first.astype(jnp.float32), second.astype(jnp.float32), (((dim_first,), (dim_second,)), ((), ())), precision=HIGHEST, preferred_element_type=jnp.float32)

def start_rows(rank, width):
    freq = lax.broadcasted_iota(jnp.int32, (rank, width), 0) + 1
    cell = 2 * lax.broadcasted_iota(jnp.int32, (rank, width), 1) + 1
    phase = freq * cell % (4 * width)
    return jnp.cos(phase.astype(jnp.float32) * (math.pi / (2 * width)))

def orthonormal(rows_t):
    gram = cross(rows_t, rows_t, 1, 1)
    shift = 1e-05 * jnp.trace(gram) / gram.shape[0] + 1e-06
    gram = gram + shift * jnp.eye(gram.shape[0], dtype=gram.dtype)
    lower = lax.linalg.cholesky(gram)
    return lax.linalg.triangular_solve(lower, rows_t, left_side=True, lower=True)

def compress(left_t, right_t):
    probe = start_rows(RK, NB)
    for sweep in range(2):
        first = cross(left_t, probe, 1, 1)
        image = orthonormal(cross(first, right_t, 0, 0))
        second = cross(right_t, image, 1, 1)
        probe = orthonormal(cross(second, left_t, 0, 0))
    first = cross(left_t, probe, 1, 1)
    return (probe, cross(first, right_t, 0, 0))

def slot_term(outer_left, inner_left, rank_l, inner_right, rank_r):
    inner = lax.dot_general(inner_left.astype(jnp.float32), inner_right.astype(jnp.float32), (((1,), (1,)), ((), ())), preferred_element_type=jnp.float32)
    index = jnp.arange(RK)
    keep = (index[:, None] < rank_l) & (index[None, :] < rank_r)
    inner = jnp.where(keep, inner, 0.0).astype(jnp.bfloat16)
    return lax.dot_general(inner.astype(jnp.float32), outer_left.astype(jnp.float32), (((0,), (0,)), ((), ())), preferred_element_type=jnp.float32)

def reference(tile_left, tile_right, left_u, left_v, rank_left, right_u, right_v, rank_right, triples):

    def one_tile(flat):
        row = flat // NTC
        col = flat % NTC
        results = []
        for layer in range(N_DEPTH):
            terms = [tile_left[row, col] / N_DEPTH]
            bases = [tile_right[row, col]]
            for slot in range(MAXA):
                panel = triples[row, col, layer, slot]
                valid = panel >= 0
                chosen = jnp.maximum(panel, 0)
                term = slot_term(left_u[layer, chosen, row], left_v[layer, chosen, row], rank_left[layer, chosen, row], right_v[layer, chosen, col], rank_right[layer, chosen, col])
                terms.append(jnp.where(valid, -term, 0.0))
                bases.append(jnp.where(valid, right_u[layer, chosen, col].astype(jnp.float32), 0.0))
            results.append(compress(jnp.concatenate(terms, axis=0), jnp.concatenate(bases, axis=0)))
        while len(results) > 1:
            joined = []
            for pair in range(len(results) // 2):
                lower_item = results[2 * pair]
                upper_item = results[2 * pair + 1]
                joined.append(compress(jnp.concatenate([lower_item[0], upper_item[0]], axis=0), jnp.concatenate([lower_item[1], upper_item[1]], axis=0)))
            results = joined
        probe, image = results[0]
        return (probe * math.sqrt(NB), image / math.sqrt(NB))
    lefts, rights = lax.map(one_tile, jnp.arange(NTR * NTC))
    return (lefts.reshape(NTR, NTC, RK, NB), rights.reshape(NTR, NTC, RK, NB))
```

```python
import math

import jax
import jax.numpy as jnp
import ml_dtypes
import numpy as np
from jax import lax
from jax.experimental import pallas as pl
from jax.experimental.pallas import tpu as pltpu
from jax.sharding import PartitionSpec as P

HIGHEST = lax.Precision.HIGHEST
LANES = 128
SUB = 8


def dot(first, second, dims=(1, 0), precision=HIGHEST):
    return lax.dot_general(
        first,
        second,
        (((dims[0],), (dims[1],)), ((), ())),
        precision=precision,
        preferred_element_type=jnp.float32,
    )


def start_table(rank, width):
    freq = np.arange(1, rank + 1, dtype=np.int64)[:, None]
    cell = 2 * np.arange(width, dtype=np.int64)[None, :] + 1
    table = np.cos((freq * cell % (4 * width)) * (math.pi / (2 * width))).astype(np.float32)
    high = table.astype(ml_dtypes.bfloat16)
    low = (table - high.astype(np.float32)).astype(ml_dtypes.bfloat16)
    return np.concatenate([high, low], axis=0)


def split(value):
    high = value.astype(jnp.bfloat16)
    return high, (value - high.astype(jnp.float32)).astype(jnp.bfloat16)


def inverse_factor(image, coeff):
    rank = coeff.shape[0]
    wide = dot(image, jnp.concatenate([coeff, coeff], axis=0), (1, 1))
    row = lax.broadcasted_iota(jnp.int32, wide.shape, 0)
    lane = lax.broadcasted_iota(jnp.int32, wide.shape, 1)
    diag = lane == row + rank
    trace = jnp.sum(jnp.where(diag, wide, 0.0))
    shift = 1e-05 * trace / rank + 1e-06
    work = jnp.where(
        lane >= rank,
        wide + jnp.where(diag, shift, 0.0),
        jnp.where(lane == row, 1.0, 0.0),
    )
    count = rank // SUB
    blocks = [work[SUB * b : SUB * (b + 1)] for b in range(count)]
    below = lax.broadcasted_iota(jnp.int32, (SUB, 2 * rank), 0)
    for p in range(count):
        cols = [
            {
                b: jnp.broadcast_to(
                    blocks[b][:, rank + SUB * p + t : rank + SUB * p + t + 1], (SUB, 2 * rank)
                )
                for b in range(p, count)
            }
            for t in range(SUB)
        ]
        for t in range(SUB):
            inverse = 1.0 / cols[t][p][t : t + 1]
            factor = {b: cols[t][b] * inverse for b in range(p, count)}
            factor[p] = jnp.where(below > t, factor[p], 0.0)
            for u in range(t + 1, SUB):
                top = cols[u][p][t : t + 1]
                for b in range(p, count):
                    cols[u][b] = cols[u][b] - factor[b] * top
            lead = blocks[p][t : t + 1]
            for b in range(p, count):
                blocks[b] = blocks[b] - factor[b] * lead
    work = jnp.concatenate(blocks, axis=0)
    pivots = jnp.sum(jnp.where(diag, work, 0.0), axis=1, keepdims=True)
    return (work / jnp.sqrt(pivots))[:, :rank]


def sweeps(seen, gram_left, gram_right, to_right, to_left):
    for _ in range(2):
        coeff = to_right(seen)
        image = dot(coeff, gram_right)
        seen = dot(inverse_factor(image, coeff), image)
        coeff = to_left(seen)
        image = dot(coeff, gram_left)
        inverse = inverse_factor(image, coeff)
        seen = dot(inverse, image)
    return dot(inverse, coeff), to_right(seen)


def layer_kernel(layers, triples, tl, tr, inner, table, lu, ru, out, xs, ys, kmat, sems):
    rank = tl.shape[0]
    slots = triples.shape[0]
    copies = []
    for slot in range(slots):
        chosen = jnp.maximum(triples[slot], 0)
        place = pl.ds((2 + slot) * rank, rank)
        for side, (src, dst) in enumerate(((lu, xs), (ru, ys))):
            copy = pltpu.make_async_copy(src.at[chosen], dst.at[place], sems.at[side, slot])
            copy.start()
            copies.append(copy)
    for src, dst in ((tl, xs), (tr, ys)):
        high, low = split(src[...])
        dst[pl.ds(0, rank)] = high
        dst[pl.ds(rank, rank)] = low
    shape = (rank, 2 * rank)
    row = lax.broadcasted_iota(jnp.int32, shape, 0)
    lane = lax.broadcasted_iota(jnp.int32, shape, 1)
    pair = jnp.where((lane == row) | (lane == row + rank), 1.0 / layers, 0.0)
    kmat[0, pl.ds(0, rank)] = pair
    kmat[0, pl.ds(rank, rank)] = pair
    for slot in range(slots):
        panel = triples[slot]
        valid = jnp.where(panel >= 0, -1.0, 0.0)
        block = inner[jnp.maximum(panel, 0)].astype(jnp.float32) * valid
        half = slot % 2
        mine = (lane >= rank) if half else (lane < rank)
        kmat[1 + slot // 2, pl.ds(half * rank, rank)] = jnp.where(mine, block, 0.0)
    for copy in copies:
        copy.wait()
    left = xs[...]
    right = ys[...]
    gram_left = dot(left, left, (1, 1), None)
    gram_right = dot(right, right, (1, 1), None)
    seen = dot(table[...], left, (1, 1), None)
    seen = seen[:rank] + seen[rank:]
    pairs = kmat.shape[0]

    def to_right(value):
        return jnp.concatenate(
            [dot(value[:, LANES * b : LANES * (b + 1)], kmat[b]) for b in range(pairs)], axis=1
        )

    def to_left(value):
        return jnp.concatenate(
            [dot(value[:, LANES * b : LANES * (b + 1)], kmat[b], (1, 1)) for b in range(pairs)],
            axis=1,
        )

    probe, image = sweeps(seen, gram_left, gram_right, to_right, to_left)
    for index, (coeff, stack) in enumerate(((probe, xs), (image, ys))):
        both = dot(jnp.concatenate(split(coeff), axis=0), stack[...], (1, 0), None)
        out[index] = both[:rank] + both[rank:]


def join_kernel(share, upper, mine, other, table, new_left, new_right):
    rank = mine.shape[1]
    width = mine.shape[2]
    is_upper = upper[0] == 1
    stacks = []
    for index in range(2):
        a, b = mine[index], other[index]
        stacks.append(
            jnp.concatenate([jnp.where(is_upper, b, a), jnp.where(is_upper, a, b)], axis=0)
        )
    left, right = stacks
    gram_left = dot(left, left, (1, 1))
    gram_right = dot(right, right, (1, 1))
    start = table[pl.ds(0, rank)].astype(jnp.float32) + table[pl.ds(rank, rank)].astype(jnp.float32)
    seen = dot(start, left, (1, 1))
    probe, image = sweeps(seen, gram_left, gram_right, lambda v: v, lambda v: v)
    scale = math.sqrt(width)
    left = jnp.where(is_upper, left[:, share:], left[:, :share])
    right = jnp.where(is_upper, right[:, share:], right[:, :share])
    new_left[0, 0] = dot(probe, left) * scale
    new_right[0, 0] = dot(image, right) / scale


def gathered(left_u, left_v, rank_left, right_u, right_v, rank_right):
    row_u, row_v, row_rank = (
        lax.all_gather(x, "cols", axis=1, tiled=True)[0, :, 0] for x in (left_u, left_v, rank_left)
    )
    col_u, col_v, col_rank = (
        lax.all_gather(x, "rows", axis=1, tiled=True)[0, :, 0]
        for x in (right_u, right_v, rank_right)
    )
    rank = row_v.shape[1]
    index = jnp.arange(rank)
    inner = jnp.einsum("kan,kbn->kab", row_v, col_v, preferred_element_type=jnp.float32)
    keep = (index[None, :, None] < row_rank[:, None, None]) & (
        index[None, None, :] < col_rank[:, None, None]
    )
    inner = jnp.where(keep, inner, 0.0).astype(jnp.bfloat16)
    return row_u, col_u, jnp.concatenate([inner, inner], axis=2)


def shards(tile_left, tile_right, left_u, left_v, rank_left, right_u, right_v, rank_right, triples):
    layers = lax.axis_size("depth")
    rank, width = tile_left.shape[2:]
    slots = triples.shape[3]
    share = width // layers
    row_u, col_u, inner = gathered(left_u, left_v, rank_left, right_u, right_v, rank_right)
    table = jnp.asarray(start_table(rank, width))
    smem = pl.BlockSpec(memory_space=pltpu.SMEM)
    vmem = pl.BlockSpec(memory_space=pltpu.VMEM)
    hbm = pl.BlockSpec(memory_space=pl.ANY)
    stack = (2 + slots) * rank
    params = pltpu.CompilerParams(vmem_limit_bytes=56 * 2**20)
    factors = pl.pallas_call(
        lambda *refs: layer_kernel(layers, *refs),
        out_shape=jax.ShapeDtypeStruct((2, rank, width), jnp.float32),
        in_specs=[smem, vmem, vmem, vmem, vmem, hbm, hbm],
        out_specs=vmem,
        scratch_shapes=[
            pltpu.VMEM((stack, width), jnp.bfloat16),
            pltpu.VMEM((stack, width), jnp.bfloat16),
            pltpu.VMEM((stack // LANES, LANES, LANES), jnp.float32),
            pltpu.SemaphoreType.DMA((2, slots)),
        ],
        compiler_params=params,
        name="layer",
    )(triples[0, 0, 0], tile_left[0, 0], tile_right[0, 0], inner, table, row_u, col_u)
    other = lax.ppermute(factors, "depth", [(d, d ^ 1) for d in range(layers)])
    upper = lax.axis_index("depth").astype(jnp.int32).reshape(1)
    out = jax.ShapeDtypeStruct((1, 1, rank, share), jnp.float32)
    return pl.pallas_call(
        lambda *refs: join_kernel(share, *refs),
        out_shape=(out, out),
        in_specs=[smem, vmem, vmem, vmem],
        out_specs=(vmem, vmem),
        compiler_params=params,
        name="join",
    )(upper, factors, other, table)


def solution(mesh):
    in_specs = (
        P("rows", "cols", None, None),
        P("rows", "cols", None, None),
        P("depth", "cols", "rows", None, None),
        P("depth", "cols", "rows", None, None),
        P("depth", "cols", "rows"),
        P("depth", "rows", "cols", None, None),
        P("depth", "rows", "cols", None, None),
        P("depth", "rows", "cols"),
        P("rows", "cols", "depth", None),
    )
    out_specs = (P("rows", "cols", None, "depth"), P("rows", "cols", None, "depth"))
    return jax.shard_map(shards, mesh=mesh, in_specs=in_specs, out_specs=out_specs, check_vma=False)
```

```python
import math

import jax
import jax.numpy as jnp
import ml_dtypes
import numpy as np
from jax import lax
from jax.experimental import pallas as pl
from jax.experimental.pallas import tpu as pltpu
from jax.sharding import PartitionSpec as P

HIGHEST = lax.Precision.HIGHEST
LANES = 128
SUB = 8


def dot(first, second, dims=(1, 0), precision=HIGHEST):
    return lax.dot_general(
        first,
        second,
        (((dims[0],), (dims[1],)), ((), ())),
        precision=precision,
        preferred_element_type=jnp.float32,
    )


def start_table(rank, width):
    freq = np.arange(1, rank + 1, dtype=np.int64)[:, None]
    cell = 2 * np.arange(width, dtype=np.int64)[None, :] + 1
    table = np.cos((freq * cell % (4 * width)) * (math.pi / (2 * width))).astype(np.float32)
    high = table.astype(ml_dtypes.bfloat16)
    low = (table - high.astype(np.float32)).astype(ml_dtypes.bfloat16)
    return np.concatenate([high, low], axis=0)


def split(value):
    high = value.astype(jnp.bfloat16)
    return high, (value - high.astype(jnp.float32)).astype(jnp.bfloat16)


def inverse_factor(image, coeff):
    rank = coeff.shape[0]
    wide = dot(image, jnp.concatenate([coeff, coeff], axis=0), (1, 1))
    row = lax.broadcasted_iota(jnp.int32, wide.shape, 0)
    lane = lax.broadcasted_iota(jnp.int32, wide.shape, 1)
    diag = lane == row + rank
    trace = jnp.sum(jnp.where(diag, wide, 0.0))
    shift = 1e-05 * trace / rank + 1e-06
    work = jnp.where(
        lane >= rank,
        wide + jnp.where(diag, shift, 0.0),
        jnp.where(lane == row, 1.0, 0.0),
    )
    count = rank // SUB
    blocks = [work[SUB * b : SUB * (b + 1)] for b in range(count)]
    below = lax.broadcasted_iota(jnp.int32, (SUB, 2 * rank), 0)
    for p in range(count):
        cols = [
            {
                b: jnp.broadcast_to(
                    blocks[b][:, rank + SUB * p + t : rank + SUB * p + t + 1], (SUB, 2 * rank)
                )
                for b in range(p, count)
            }
            for t in range(SUB)
        ]
        for t in range(SUB):
            inverse = 1.0 / cols[t][p][t : t + 1]
            factor = {b: cols[t][b] * inverse for b in range(p, count)}
            factor[p] = jnp.where(below > t, factor[p], 0.0)
            for u in range(t + 1, SUB):
                top = cols[u][p][t : t + 1]
                for b in range(p, count):
                    cols[u][b] = cols[u][b] - factor[b] * top
            lead = blocks[p][t : t + 1]
            for b in range(p, count):
                blocks[b] = blocks[b] - factor[b] * lead
    work = jnp.concatenate(blocks, axis=0)
    pivots = jnp.sum(jnp.where(diag, work, 0.0), axis=1, keepdims=True)
    return (work / jnp.sqrt(pivots))[:, :rank]


def sweeps(seen, gram_left, gram_right, to_right, to_left):
    for _ in range(2):
        coeff = to_right(seen)
        image = dot(coeff, gram_right)
        seen = dot(inverse_factor(image, coeff), image)
        coeff = to_left(seen)
        image = dot(coeff, gram_left)
        inverse = inverse_factor(image, coeff)
        seen = dot(inverse, image)
    return dot(inverse, coeff), to_right(seen)


def layer_kernel(layers, triples, tl, tr, inner, table, lu, ru, out, xs, ys, kmat, sems):
    rank = tl.shape[0]
    slots = triples.shape[0]
    copies = []
    for slot in range(slots):
        chosen = jnp.maximum(triples[slot], 0)
        place = pl.ds((2 + slot) * rank, rank)
        for side, (src, dst) in enumerate(((lu, xs), (ru, ys))):
            copy = pltpu.make_async_copy(src.at[chosen], dst.at[place], sems.at[side, slot])
            copy.start()
            copies.append(copy)
    for src, dst in ((tl, xs), (tr, ys)):
        high, low = split(src[...])
        dst[pl.ds(0, rank)] = high
        dst[pl.ds(rank, rank)] = low
    shape = (rank, 2 * rank)
    row = lax.broadcasted_iota(jnp.int32, shape, 0)
    lane = lax.broadcasted_iota(jnp.int32, shape, 1)
    pair = jnp.where((lane == row) | (lane == row + rank), 1.0 / layers, 0.0)
    kmat[0, pl.ds(0, rank)] = pair
    kmat[0, pl.ds(rank, rank)] = pair
    for slot in range(slots):
        panel = triples[slot]
        valid = jnp.where(panel >= 0, -1.0, 0.0)
        block = inner[jnp.maximum(panel, 0)].astype(jnp.float32) * valid
        half = slot % 2
        mine = (lane >= rank) if half else (lane < rank)
        kmat[1 + slot // 2, pl.ds(half * rank, rank)] = jnp.where(mine, block, 0.0)
    for copy in copies:
        copy.wait()
    left = xs[...]
    right = ys[...]
    gram_left = dot(left, left, (1, 1), None)
    gram_right = dot(right, right, (1, 1), None)
    seen = dot(table[...], left, (1, 1), None)
    seen = seen[:rank] + seen[rank:]
    pairs = kmat.shape[0]

    def to_right(value):
        return jnp.concatenate(
            [dot(value[:, LANES * b : LANES * (b + 1)], kmat[b]) for b in range(pairs)], axis=1
        )

    def to_left(value):
        return jnp.concatenate(
            [dot(value[:, LANES * b : LANES * (b + 1)], kmat[b], (1, 1)) for b in range(pairs)],
            axis=1,
        )

    probe, image = sweeps(seen, gram_left, gram_right, to_right, to_left)
    for index, (coeff, stack) in enumerate(((probe, xs), (image, ys))):
        both = dot(jnp.concatenate(split(coeff), axis=0), stack[...], (1, 0), None)
        out[index] = both[:rank] + both[rank:]


def join_kernel(share, upper, mine, other, table, new_left, new_right):
    rank = mine.shape[1]
    width = mine.shape[2]
    is_upper = upper[0] == 1
    stacks = []
    for index in range(2):
        a, b = mine[index], other[index]
        stacks.append(
            jnp.concatenate([jnp.where(is_upper, b, a), jnp.where(is_upper, a, b)], axis=0)
        )
    left, right = stacks
    gram_left = dot(left, left, (1, 1))
    gram_right = dot(right, right, (1, 1))
    start = table[pl.ds(0, rank)].astype(jnp.float32) + table[pl.ds(rank, rank)].astype(jnp.float32)
    seen = dot(start, left, (1, 1))
    probe, image = sweeps(seen, gram_left, gram_right, lambda v: v, lambda v: v)
    scale = math.sqrt(width)
    left = jnp.where(is_upper, left[:, share:], left[:, :share])
    right = jnp.where(is_upper, right[:, share:], right[:, :share])
    new_left[0, 0] = dot(probe, left) * scale
    new_right[0, 0] = dot(image, right) / scale


def gathered(left_u, left_v, rank_left, right_u, right_v, rank_right):
    row_u, row_v, row_rank = (
        lax.all_gather(x, "cols", axis=1, tiled=True)[0, :, 0] for x in (left_u, left_v, rank_left)
    )
    col_u, col_v, col_rank = (
        lax.all_gather(x, "rows", axis=1, tiled=True)[0, :, 0]
        for x in (right_u, right_v, rank_right)
    )
    rank = row_v.shape[1]
    index = jnp.arange(rank)
    inner = jnp.einsum("kan,kbn->kab", row_v, col_v, preferred_element_type=jnp.float32)
    keep = (index[None, :, None] < row_rank[:, None, None]) & (
        index[None, None, :] < col_rank[:, None, None]
    )
    inner = jnp.where(keep, inner, 0.0).astype(jnp.bfloat16)
    return row_u, col_u, jnp.concatenate([inner, inner], axis=2)


MESH = pl.DeviceIdType.MESH


def panels_kernel(n_r, n_c, lu, lv, ru, rv, lu_all, ru_all, inner_all, lv_in, rv_in, own,
                  local_sem, rv_send, rv_recv, lv_send, lv_recv, lu_send, lu_recv,
                  ru_send, ru_recv, right_send, left_send, in_send, in_recv):
    r = lax.axis_index("rows")
    c = lax.axis_index("cols")
    d = lax.axis_index("depth")
    total = n_r * n_c
    flat = r * n_c + c
    panel = c * n_r + r
    rank = lv.shape[1]

    def remote(src, dst, send, recv, row, col):
        return pltpu.make_async_remote_copy(
            src_ref=src, dst_ref=dst, send_sem=send, recv_sem=recv,
            device_id=(row, col, d), device_id_type=MESH)

    def arrived(dst, send, recv):
        remote(dst, dst, send, recv, lax.rem(r + 1, n_r), c).wait_recv()

    barrier = pltpu.get_barrier_semaphore()
    for t in range(1, total):
        to = lax.rem(flat + t, total)
        pl.semaphore_signal(barrier, inc=1, device_id=(to // n_c, lax.rem(to, n_c), d),
                            device_id_type=MESH)
    pl.semaphore_wait(barrier, total - 1)

    rv_self = r == c

    def rv_copy(m):
        return remote(rv.at[m], rv_in.at[c], rv_send.at[m], rv_recv.at[c], m, r)

    def lv_copy(t):
        to = lax.rem(r + t, n_r)
        return remote(lv.at[to], lv_in.at[r], lv_send.at[t], lv_recv.at[r], to, c)

    def lu_copy(side):
        return remote(lu, lu_all.at[c], lu_send.at[side], lu_recv.at[c], r, c + (1 if side else -1))

    def ru_copy(t):
        return remote(ru, ru_all.at[r], ru_send.at[t], ru_recv.at[r], lax.rem(r + t, n_r), c)

    for m in range(n_r):
        @pl.when(jnp.logical_not(jnp.logical_and(rv_self, r == m)))
        def _():
            rv_copy(m).start()

    own_rv = pltpu.make_async_copy(rv.at[r], rv_in.at[c], local_sem.at[0])
    own_lv = pltpu.make_async_copy(lv.at[r], lv_in.at[r], local_sem.at[1])
    own_lu = pltpu.make_async_copy(lu, lu_all.at[c], local_sem.at[2])
    own_ru = pltpu.make_async_copy(ru, ru_all.at[r], local_sem.at[3])
    for t in range(1, n_r):
        lv_copy(t).start()

    @pl.when(c + 1 < n_c)
    def _():
        lu_copy(1).start()

    @pl.when(c > 0)
    def _():
        lu_copy(0).start()

    for t in range(1, n_r):
        ru_copy(t).start()

    @pl.when(rv_self)
    def _():
        own_rv.start()

    own_lv.start()
    own_lu.start()
    own_ru.start()

    def pass_right(t):
        s = c - t
        return remote(lu_all.at[s], lu_all.at[s], right_send.at[t], lu_recv.at[s], r, c + 1)

    def pass_left(t):
        s = c + t
        return remote(lu_all.at[s], lu_all.at[s], left_send.at[t], lu_recv.at[s], r, c - 1)

    def relay(t):
        @pl.when(c - t >= 0)
        def _():
            arrived(lu_all.at[c - t], right_send.at[t], lu_recv.at[c - t])

            @pl.when(c + 1 < n_c)
            def _():
                pass_right(t).start()

        @pl.when(c + t < n_c)
        def _():
            arrived(lu_all.at[c + t], left_send.at[t], lu_recv.at[c + t])

            @pl.when(c > 0)
            def _():
                pass_left(t).start()

    relay(1)
    for j in range(n_c):
        @pl.when(jnp.logical_not(jnp.logical_and(rv_self, c == j)))
        def _():
            arrived(rv_in.at[j], rv_send.at[0], rv_recv.at[j])

    @pl.when(rv_self)
    def _():
        own_rv.wait()

    own_lv.wait()
    for t in range(1, n_r):
        source = lax.rem(r + t, n_r)
        arrived(lv_in.at[source], lv_send.at[t], lv_recv.at[source])
    lefts = lv_in[...].reshape(n_r * rank, lv_in.shape[2])
    for j in range(n_c):
        right = rv_in[j]
        both = jnp.concatenate([right, right], axis=0)
        inner = dot(lefts, both, (1, 1), None).astype(jnp.bfloat16)
        own[j] = inner.reshape(n_r, rank, 2 * rank)

    def in_copy(t):
        to = lax.rem(flat + t, total)
        row = to // n_c
        col = lax.rem(to, n_c)
        return remote(own.at[col, row], inner_all.at[panel], in_send.at[t], in_recv.at[panel], row, col)

    for t in range(1, total):
        in_copy(t).start()
    own_inner = pltpu.make_async_copy(own.at[c, r], inner_all.at[panel], local_sem.at[4])
    own_inner.start()
    for t in range(2, n_c):
        relay(t)
    for t in range(1, n_r):
        source = lax.rem(r + t, n_r)
        arrived(ru_all.at[source], ru_send.at[t], ru_recv.at[source])
    for t in range(1, total):
        source = lax.rem(panel + t, total)
        arrived(inner_all.at[source], in_send.at[t], in_recv.at[source])
    own_inner.wait()
    own_lu.wait()
    own_ru.wait()
    for m in range(n_r):
        @pl.when(jnp.logical_not(jnp.logical_and(rv_self, r == m)))
        def _():
            rv_copy(m).wait_send()
    for t in range(1, n_r):
        lv_copy(t).wait_send()
        ru_copy(t).wait_send()

    @pl.when(c + 1 < n_c)
    def _():
        lu_copy(1).wait_send()

    @pl.when(c > 0)
    def _():
        lu_copy(0).wait_send()

    for t in range(1, n_c):
        @pl.when(jnp.logical_and(c - t >= 0, c + 1 < n_c))
        def _():
            pass_right(t).wait_send()

        @pl.when(jnp.logical_and(c + t < n_c, c > 0))
        def _():
            pass_left(t).wait_send()
    for t in range(1, total):
        in_copy(t).wait_send()


def exchanged(left_u, left_v, rank_left, right_u, right_v, rank_right):
    n_r = lax.axis_size("rows")
    n_c = lax.axis_size("cols")
    lu, lv, rl = (x[0, :, 0] for x in (left_u, left_v, rank_left))
    ru, rv, rr = (x[0, :, 0] for x in (right_u, right_v, rank_right))
    rank, width = lu.shape[1:]
    index = jnp.arange(rank)
    lv = jnp.where((index[None, :] < rl[:, None])[:, :, None], lv, 0)
    rv = jnp.where((index[None, :] < rr[:, None])[:, :, None], rv, 0)
    hbm = pl.BlockSpec(memory_space=pl.ANY)
    total = n_r * n_c
    bf16 = jnp.bfloat16
    dma = pltpu.SemaphoreType.DMA
    lu_all, ru_all, inner = pl.pallas_call(
        lambda *refs: panels_kernel(n_r, n_c, *refs),
        out_shape=(
            jax.ShapeDtypeStruct((n_c,) + lu.shape, bf16),
            jax.ShapeDtypeStruct((n_r,) + ru.shape, bf16),
            jax.ShapeDtypeStruct((total, rank, 2 * rank), bf16),
        ),
        in_specs=[hbm] * 4,
        out_specs=(hbm, hbm, hbm),
        scratch_shapes=[
            pltpu.VMEM((n_r, rank, width), bf16),
            pltpu.VMEM((n_c, rank, width), bf16),
            pltpu.VMEM((n_c, n_r, rank, 2 * rank), bf16),
            dma((5,)),
            dma((n_r,)), dma((n_c,)), dma((n_r,)), dma((n_r,)),
            dma((2,)), dma((n_c,)), dma((n_r,)), dma((n_r,)),
            dma((n_c,)), dma((n_c,)), dma((total,)), dma((total,)),
        ],
        compiler_params=pltpu.CompilerParams(
            collective_id=0, has_side_effects=True, vmem_limit_bytes=56 * 2**20),
        name="panels",
    )(lu, lv, ru, rv)
    return (lu_all.reshape(total, rank, width), ru_all.reshape(total, rank, width), inner)


def shards(tile_left, tile_right, left_u, left_v, rank_left, right_u, right_v, rank_right, triples):
    layers = lax.axis_size("depth")
    rank, width = tile_left.shape[2:]
    slots = triples.shape[3]
    share = width // layers
    sizes = {lax.axis_size("rows"), lax.axis_size("cols"), left_u.shape[1], right_u.shape[1]}
    bring = exchanged if len(sizes) == 1 else gathered
    row_u, col_u, inner = bring(left_u, left_v, rank_left, right_u, right_v, rank_right)
    table = jnp.asarray(start_table(rank, width))
    smem = pl.BlockSpec(memory_space=pltpu.SMEM)
    vmem = pl.BlockSpec(memory_space=pltpu.VMEM)
    hbm = pl.BlockSpec(memory_space=pl.ANY)
    stack = (2 + slots) * rank
    params = pltpu.CompilerParams(vmem_limit_bytes=56 * 2**20)
    factors = pl.pallas_call(
        lambda *refs: layer_kernel(layers, *refs),
        out_shape=jax.ShapeDtypeStruct((2, rank, width), jnp.float32),
        in_specs=[smem, vmem, vmem, vmem, vmem, hbm, hbm],
        out_specs=vmem,
        scratch_shapes=[
            pltpu.VMEM((stack, width), jnp.bfloat16),
            pltpu.VMEM((stack, width), jnp.bfloat16),
            pltpu.VMEM((stack // LANES, LANES, LANES), jnp.float32),
            pltpu.SemaphoreType.DMA((2, slots)),
        ],
        compiler_params=params,
        name="layer",
    )(triples[0, 0, 0], tile_left[0, 0], tile_right[0, 0], inner, table, row_u, col_u)
    other = lax.ppermute(factors, "depth", [(d, d ^ 1) for d in range(layers)])
    upper = lax.axis_index("depth").astype(jnp.int32).reshape(1)
    out = jax.ShapeDtypeStruct((1, 1, rank, share), jnp.float32)
    return pl.pallas_call(
        lambda *refs: join_kernel(share, *refs),
        out_shape=(out, out),
        in_specs=[smem, vmem, vmem, vmem],
        out_specs=(vmem, vmem),
        compiler_params=params,
        name="join",
    )(upper, factors, other, table)


def solution(mesh):
    in_specs = (
        P("rows", "cols", None, None),
        P("rows", "cols", None, None),
        P("depth", "cols", "rows", None, None),
        P("depth", "cols", "rows", None, None),
        P("depth", "cols", "rows"),
        P("depth", "rows", "cols", None, None),
        P("depth", "rows", "cols", None, None),
        P("depth", "rows", "cols"),
        P("rows", "cols", "depth", None),
    )
    out_specs = (P("rows", "cols", None, "depth"), P("rows", "cols", None, "depth"))
    return jax.shard_map(shards, mesh=mesh, in_specs=in_specs, out_specs=out_specs, check_vma=False)
```

```python
import math

import jax
import jax.numpy as jnp
import ml_dtypes
import numpy as np
from jax import lax
from jax.experimental import pallas as pl
from jax.experimental.pallas import tpu as pltpu
from jax.sharding import PartitionSpec as P

HIGHEST = lax.Precision.HIGHEST
LANES = 128
SUB = 8


def dot(first, second, dims=(1, 0), precision=HIGHEST):
    return lax.dot_general(
        first,
        second,
        (((dims[0],), (dims[1],)), ((), ())),
        precision=precision,
        preferred_element_type=jnp.float32,
    )


def start_table(rank, width):
    freq = np.arange(1, rank + 1, dtype=np.int64)[:, None]
    cell = 2 * np.arange(width, dtype=np.int64)[None, :] + 1
    table = np.cos((freq * cell % (4 * width)) * (math.pi / (2 * width))).astype(np.float32)
    high = table.astype(ml_dtypes.bfloat16)
    low = (table - high.astype(np.float32)).astype(ml_dtypes.bfloat16)
    return np.concatenate([high, low], axis=0)


def split(value):
    high = value.astype(jnp.bfloat16)
    return high, (value - high.astype(jnp.float32)).astype(jnp.bfloat16)


def thirds(value):
    first, rest = value.astype(jnp.bfloat16), value
    rest = rest - first.astype(jnp.float32)
    second = rest.astype(jnp.bfloat16)
    return first, second, (rest - second.astype(jnp.float32)).astype(jnp.bfloat16)


def dot_pieces(value, pieces):
    rows = value.shape[0]
    parts = thirds(value)
    total = None
    for index in (2, 1, 0):
        both = dot(jnp.concatenate(parts[: 3 - index], axis=0), pieces[index], (1, 0), None)
        for part in reversed(range(3 - index)):
            term = both[rows * part : rows * (part + 1)]
            total = term if total is None else total + term
    return total


def inverse_factor(image, coeff):
    rank = coeff.shape[0]
    wide = dot(image, jnp.concatenate([coeff, coeff], axis=0), (1, 1))
    row = lax.broadcasted_iota(jnp.int32, wide.shape, 0)
    lane = lax.broadcasted_iota(jnp.int32, wide.shape, 1)
    diag = lane == row + rank
    trace = jnp.sum(jnp.where(diag, wide, 0.0))
    shift = 1e-05 * trace / rank + 1e-06
    work = jnp.where(
        lane >= rank,
        wide + jnp.where(diag, shift, 0.0),
        jnp.where(lane == row, 1.0, 0.0),
    )
    count = rank // SUB
    blocks = [work[SUB * b : SUB * (b + 1)] for b in range(count)]
    below = lax.broadcasted_iota(jnp.int32, (SUB, 2 * rank), 0)
    for p in range(count):
        cols = [
            {
                b: jnp.broadcast_to(
                    blocks[b][:, rank + SUB * p + t : rank + SUB * p + t + 1], (SUB, 2 * rank)
                )
                for b in range(p, count)
            }
            for t in range(SUB)
        ]
        for t in range(SUB):
            inverse = 1.0 / cols[t][p][t : t + 1]
            factor = {b: cols[t][b] * inverse for b in range(p, count)}
            factor[p] = jnp.where(below > t, factor[p], 0.0)
            for u in range(t + 1, SUB):
                top = cols[u][p][t : t + 1]
                for b in range(p, count):
                    cols[u][b] = cols[u][b] - factor[b] * top
            lead = blocks[p][t : t + 1]
            for b in range(p, count):
                blocks[b] = blocks[b] - factor[b] * lead
    work = jnp.concatenate(blocks, axis=0)
    pivots = jnp.sum(jnp.where(diag, work, 0.0), axis=1, keepdims=True)
    return (work / jnp.sqrt(pivots))[:, :rank]


def sweeps(seen, gram_left, gram_right, to_right, to_left):
    for _ in range(2):
        coeff = to_right(seen)
        image = dot_pieces(coeff, gram_right)
        seen = dot(inverse_factor(image, coeff), image)
        coeff = to_left(seen)
        image = dot_pieces(coeff, gram_left)
        inverse = inverse_factor(image, coeff)
        seen = dot(inverse, image)
    return dot(inverse, coeff), to_right(seen)


def layer_kernel(layers, triples, tl, tr, inner, table, lu, ru, out, xs, ys, kmat, sems):
    rank = tl.shape[0]
    slots = triples.shape[0]
    copies = []
    for slot in range(slots):
        chosen = jnp.maximum(triples[slot], 0)
        place = pl.ds((2 + slot) * rank, rank)
        for side, (src, dst) in enumerate(((lu, xs), (ru, ys))):
            copy = pltpu.make_async_copy(src.at[chosen], dst.at[place], sems.at[side, slot])
            copy.start()
            copies.append(copy)
    for src, dst in ((tl, xs), (tr, ys)):
        high, low = split(src[...])
        dst[pl.ds(0, rank)] = high
        dst[pl.ds(rank, rank)] = low
    shape = (rank, 2 * rank)
    row = lax.broadcasted_iota(jnp.int32, shape, 0)
    lane = lax.broadcasted_iota(jnp.int32, shape, 1)
    pair = jnp.where((lane == row) | (lane == row + rank), 1.0 / layers, 0.0)
    kmat[0, pl.ds(0, rank)] = pair
    kmat[0, pl.ds(rank, rank)] = pair
    for slot in range(slots):
        panel = triples[slot]
        valid = jnp.where(panel >= 0, -1.0, 0.0)
        block = inner[jnp.maximum(panel, 0)].astype(jnp.float32) * valid
        half = slot % 2
        mine = (lane >= rank) if half else (lane < rank)
        kmat[1 + slot // 2, pl.ds(half * rank, rank)] = jnp.where(mine, block, 0.0)
    for copy in copies:
        copy.wait()
    left = xs[...]
    right = ys[...]
    gram_left = thirds(dot(left, left, (1, 1), None))
    gram_right = thirds(dot(right, right, (1, 1), None))
    seen = dot(table[...], left, (1, 1), None)
    seen = seen[:rank] + seen[rank:]
    pairs = kmat.shape[0]

    def to_right(value):
        return jnp.concatenate(
            [dot(value[:, LANES * b : LANES * (b + 1)], kmat[b]) for b in range(pairs)], axis=1
        )

    def to_left(value):
        return jnp.concatenate(
            [dot(value[:, LANES * b : LANES * (b + 1)], kmat[b], (1, 1)) for b in range(pairs)],
            axis=1,
        )

    probe, image = sweeps(seen, gram_left, gram_right, to_right, to_left)
    for index, (coeff, stack) in enumerate(((probe, xs), (image, ys))):
        both = dot(jnp.concatenate(split(coeff), axis=0), stack[...], (1, 0), None)
        out[index] = both[:rank] + both[rank:]


def join_kernel(share, upper, mine, other, table, new_left, new_right):
    rank = mine.shape[1]
    width = mine.shape[2]
    is_upper = upper[0] == 1
    both = 2 * rank
    stacks = []
    for index in range(2):
        a, b = mine[index], other[index]
        value = jnp.concatenate([jnp.where(is_upper, b, a), jnp.where(is_upper, a, b)], axis=0)
        stacks.append(jnp.concatenate(split(value), axis=0))
    left, right = stacks

    def folded(stack):
        gram = dot(stack, stack, (1, 1), None)
        gram = gram[:both] + gram[both:]
        return thirds(gram[:, :both] + gram[:, both:])

    seen = dot(table[...], left, (1, 1), None)
    seen = seen[:rank] + seen[rank:]
    seen = seen[:, :both] + seen[:, both:]
    probe, image = sweeps(seen, folded(left), folded(right), lambda v: v, lambda v: v)
    scale = math.sqrt(width)

    def expand(coeff, stack):
        pieces = jnp.concatenate(split(coeff), axis=0)
        half = jnp.where(is_upper, stack[:, share:], stack[:, :share])
        out = dot(jnp.concatenate([pieces, pieces], axis=1), half, (1, 0), None)
        return out[:rank] + out[rank:]

    new_left[0, 0] = expand(probe, left) * scale
    new_right[0, 0] = expand(image, right) / scale


def gathered(left_u, left_v, rank_left, right_u, right_v, rank_right):
    row_u, row_v, row_rank = (
        lax.all_gather(x, "cols", axis=1, tiled=True)[0, :, 0] for x in (left_u, left_v, rank_left)
    )
    col_u, col_v, col_rank = (
        lax.all_gather(x, "rows", axis=1, tiled=True)[0, :, 0]
        for x in (right_u, right_v, rank_right)
    )
    rank = row_v.shape[1]
    index = jnp.arange(rank)
    inner = jnp.einsum("kan,kbn->kab", row_v, col_v, preferred_element_type=jnp.float32)
    keep = (index[None, :, None] < row_rank[:, None, None]) & (
        index[None, None, :] < col_rank[:, None, None]
    )
    inner = jnp.where(keep, inner, 0.0).astype(jnp.bfloat16)
    return row_u, col_u, jnp.concatenate([inner, inner], axis=2)


MESH = pl.DeviceIdType.MESH


def panels_kernel(n_r, n_c, lu, lv, ru, rv, lu_all, ru_all, inner_all, lv_in, rv_in, own,
                  local_sem, rv_send, rv_recv, lv_send, lv_recv, lu_send, lu_recv,
                  ru_send, ru_recv, right_send, left_send, in_send, in_recv):
    r = lax.axis_index("rows")
    c = lax.axis_index("cols")
    d = lax.axis_index("depth")
    total = n_r * n_c
    flat = r * n_c + c
    panel = c * n_r + r
    rank = lv.shape[1]

    def remote(src, dst, send, recv, row, col):
        return pltpu.make_async_remote_copy(
            src_ref=src, dst_ref=dst, send_sem=send, recv_sem=recv,
            device_id=(row, col, d), device_id_type=MESH)

    def arrived(dst, send, recv):
        remote(dst, dst, send, recv, lax.rem(r + 1, n_r), c).wait_recv()

    barrier = pltpu.get_barrier_semaphore()
    for t in range(1, total):
        to = lax.rem(flat + t, total)
        pl.semaphore_signal(barrier, inc=1, device_id=(to // n_c, lax.rem(to, n_c), d),
                            device_id_type=MESH)
    pl.semaphore_wait(barrier, total - 1)

    rv_self = r == c

    def rv_copy(m):
        return remote(rv.at[m], rv_in.at[c], rv_send.at[m], rv_recv.at[c], m, r)

    def lv_copy(t):
        to = lax.rem(r + t, n_r)
        return remote(lv.at[to], lv_in.at[r], lv_send.at[t], lv_recv.at[r], to, c)

    def lu_copy(side):
        return [
            remote(lu.at[q], lu_all.at[c, q], lu_send.at[side, q], lu_recv.at[c, q], r,
                   c + (1 if side else -1))
            for q in range(lu.shape[0])
        ]

    def ru_copy(t):
        return remote(ru, ru_all.at[r], ru_send.at[t], ru_recv.at[r], lax.rem(r + t, n_r), c)

    @pl.when(c + 1 < n_c)
    def _():
        for copy in lu_copy(1):
            copy.start()

    @pl.when(c > 0)
    def _():
        for copy in lu_copy(0):
            copy.start()

    for m in range(n_r):
        @pl.when(jnp.logical_not(jnp.logical_and(rv_self, r == m)))
        def _():
            rv_copy(m).start()

    own_rv = pltpu.make_async_copy(rv.at[r], rv_in.at[c], local_sem.at[0])
    own_lv = pltpu.make_async_copy(lv.at[r], lv_in.at[r], local_sem.at[1])
    own_lu = pltpu.make_async_copy(lu, lu_all.at[c], local_sem.at[2])
    own_ru = pltpu.make_async_copy(ru, ru_all.at[r], local_sem.at[3])
    for t in range(1, n_r):
        lv_copy(t).start()

    for t in range(1, n_r):
        ru_copy(t).start()

    @pl.when(rv_self)
    def _():
        own_rv.start()

    own_lv.start()
    own_lu.start()
    own_ru.start()

    def pass_right(t, q):
        s = c - t
        return remote(lu_all.at[s, q], lu_all.at[s, q], right_send.at[t, q], lu_recv.at[s, q], r, c + 1)

    def pass_left(t, q):
        s = c + t
        return remote(lu_all.at[s, q], lu_all.at[s, q], left_send.at[t, q], lu_recv.at[s, q], r, c - 1)

    def relay_one(t, q):
        @pl.when(c - t >= 0)
        def _():
            arrived(lu_all.at[c - t, q], right_send.at[t, q], lu_recv.at[c - t, q])

            @pl.when(c + 1 < n_c)
            def _():
                pass_right(t, q).start()

        @pl.when(c + t < n_c)
        def _():
            arrived(lu_all.at[c + t, q], left_send.at[t, q], lu_recv.at[c + t, q])

            @pl.when(c > 0)
            def _():
                pass_left(t, q).start()

    def relay(t):
        for q in range(lu.shape[0]):
            relay_one(t, q)

    for t in range(1, n_c - 1):
        relay(t)
    for j in range(n_c):
        @pl.when(jnp.logical_not(jnp.logical_and(rv_self, c == j)))
        def _():
            arrived(rv_in.at[j], rv_send.at[0], rv_recv.at[j])

    @pl.when(rv_self)
    def _():
        own_rv.wait()

    own_lv.wait()
    for t in range(1, n_r):
        source = lax.rem(r + t, n_r)
        arrived(lv_in.at[source], lv_send.at[t], lv_recv.at[source])
    lefts = lv_in[...].reshape(n_r * rank, lv_in.shape[2])
    for j in range(n_c):
        right = rv_in[j]
        both = jnp.concatenate([right, right], axis=0)
        inner = dot(lefts, both, (1, 1), None).astype(jnp.bfloat16)
        own[j] = inner.reshape(n_r, rank, 2 * rank)

    def in_copy(t):
        to = lax.rem(flat + t, total)
        row = to // n_c
        col = lax.rem(to, n_c)
        return remote(own.at[col, row], inner_all.at[panel], in_send.at[t], in_recv.at[panel], row, col)

    for t in range(1, total):
        in_copy(t).start()
    own_inner = pltpu.make_async_copy(own.at[c, r], inner_all.at[panel], local_sem.at[4])
    own_inner.start()
    relay(n_c - 1)
    for t in range(1, n_r):
        source = lax.rem(r + t, n_r)
        arrived(ru_all.at[source], ru_send.at[t], ru_recv.at[source])
    for t in range(1, total):
        source = lax.rem(panel + t, total)
        arrived(inner_all.at[source], in_send.at[t], in_recv.at[source])
    own_inner.wait()
    own_lu.wait()
    own_ru.wait()
    for m in range(n_r):
        @pl.when(jnp.logical_not(jnp.logical_and(rv_self, r == m)))
        def _():
            rv_copy(m).wait_send()
    for t in range(1, n_r):
        lv_copy(t).wait_send()
        ru_copy(t).wait_send()

    @pl.when(c + 1 < n_c)
    def _():
        for copy in lu_copy(1):
            copy.wait_send()

    @pl.when(c > 0)
    def _():
        for copy in lu_copy(0):
            copy.wait_send()

    for t in range(1, n_c):
        @pl.when(jnp.logical_and(c - t >= 0, c + 1 < n_c))
        def _():
            for q in range(lu.shape[0]):
                pass_right(t, q).wait_send()

        @pl.when(jnp.logical_and(c + t < n_c, c > 0))
        def _():
            for q in range(lu.shape[0]):
                pass_left(t, q).wait_send()
    for t in range(1, total):
        in_copy(t).wait_send()


def exchanged(left_u, left_v, rank_left, right_u, right_v, rank_right):
    n_r = lax.axis_size("rows")
    n_c = lax.axis_size("cols")
    lu, lv, rl = (x[0, :, 0] for x in (left_u, left_v, rank_left))
    ru, rv, rr = (x[0, :, 0] for x in (right_u, right_v, rank_right))
    rank, width = lu.shape[1:]
    index = jnp.arange(rank)
    lv = jnp.where((index[None, :] < rl[:, None])[:, :, None], lv, 0)
    rv = jnp.where((index[None, :] < rr[:, None])[:, :, None], rv, 0)
    hbm = pl.BlockSpec(memory_space=pl.ANY)
    total = n_r * n_c
    per = lu.shape[0]
    bf16 = jnp.bfloat16
    dma = pltpu.SemaphoreType.DMA
    lu_all, ru_all, inner = pl.pallas_call(
        lambda *refs: panels_kernel(n_r, n_c, *refs),
        out_shape=(
            jax.ShapeDtypeStruct((n_c,) + lu.shape, bf16),
            jax.ShapeDtypeStruct((n_r,) + ru.shape, bf16),
            jax.ShapeDtypeStruct((total, rank, 2 * rank), bf16),
        ),
        in_specs=[hbm] * 4,
        out_specs=(hbm, hbm, hbm),
        scratch_shapes=[
            pltpu.VMEM((n_r, rank, width), bf16),
            pltpu.VMEM((n_c, rank, width), bf16),
            pltpu.VMEM((n_c, n_r, rank, 2 * rank), bf16),
            dma((5,)),
            dma((n_r,)), dma((n_c,)), dma((n_r,)), dma((n_r,)),
            dma((2, per)), dma((n_c, per)), dma((n_r,)), dma((n_r,)),
            dma((n_c, per)), dma((n_c, per)), dma((total,)), dma((total,)),
        ],
        compiler_params=pltpu.CompilerParams(
            collective_id=0, has_side_effects=True, vmem_limit_bytes=56 * 2**20),
        name="panels",
    )(lu, lv, ru, rv)
    return (lu_all.reshape(total, rank, width), ru_all.reshape(total, rank, width), inner)


def shards(tile_left, tile_right, left_u, left_v, rank_left, right_u, right_v, rank_right, triples):
    layers = lax.axis_size("depth")
    rank, width = tile_left.shape[2:]
    slots = triples.shape[3]
    share = width // layers
    sizes = {lax.axis_size("rows"), lax.axis_size("cols"), left_u.shape[1], right_u.shape[1]}
    bring = exchanged if len(sizes) == 1 else gathered
    row_u, col_u, inner = bring(left_u, left_v, rank_left, right_u, right_v, rank_right)
    table = jnp.asarray(start_table(rank, width))
    smem = pl.BlockSpec(memory_space=pltpu.SMEM)
    vmem = pl.BlockSpec(memory_space=pltpu.VMEM)
    hbm = pl.BlockSpec(memory_space=pl.ANY)
    stack = (2 + slots) * rank
    params = pltpu.CompilerParams(vmem_limit_bytes=56 * 2**20)
    factors = pl.pallas_call(
        lambda *refs: layer_kernel(layers, *refs),
        out_shape=jax.ShapeDtypeStruct((2, rank, width), jnp.float32),
        in_specs=[smem, vmem, vmem, vmem, vmem, hbm, hbm],
        out_specs=vmem,
        scratch_shapes=[
            pltpu.VMEM((stack, width), jnp.bfloat16),
            pltpu.VMEM((stack, width), jnp.bfloat16),
            pltpu.VMEM((stack // LANES, LANES, LANES), jnp.float32),
            pltpu.SemaphoreType.DMA((2, slots)),
        ],
        compiler_params=params,
        name="layer",
    )(triples[0, 0, 0], tile_left[0, 0], tile_right[0, 0], inner, table, row_u, col_u)
    other = lax.ppermute(factors, "depth", [(d, d ^ 1) for d in range(layers)])
    upper = lax.axis_index("depth").astype(jnp.int32).reshape(1)
    out = jax.ShapeDtypeStruct((1, 1, rank, share), jnp.float32)
    return pl.pallas_call(
        lambda *refs: join_kernel(share, *refs),
        out_shape=(out, out),
        in_specs=[smem, vmem, vmem, vmem],
        out_specs=(vmem, vmem),
        compiler_params=params,
        name="join",
    )(upper, factors, other, table)


def solution(mesh):
    in_specs = (
        P("rows", "cols", None, None),
        P("rows", "cols", None, None),
        P("depth", "cols", "rows", None, None),
        P("depth", "cols", "rows", None, None),
        P("depth", "cols", "rows"),
        P("depth", "rows", "cols", None, None),
        P("depth", "rows", "cols", None, None),
        P("depth", "rows", "cols"),
        P("rows", "cols", "depth", None),
    )
    out_specs = (P("rows", "cols", None, "depth"), P("rows", "cols", None, "depth"))
    return jax.shard_map(shards, mesh=mesh, in_specs=in_specs, out_specs=out_specs, check_vma=False)
```

```python
import math

import jax
import jax.numpy as jnp
import ml_dtypes
import numpy as np
from jax import lax
from jax.experimental import pallas as pl
from jax.experimental.pallas import tpu as pltpu
from jax.sharding import PartitionSpec as P

HIGHEST = lax.Precision.HIGHEST
LANES = 128
SUB = 8


def dot(first, second, dims=(1, 0), precision=HIGHEST):
    return lax.dot_general(
        first,
        second,
        (((dims[0],), (dims[1],)), ((), ())),
        precision=precision,
        preferred_element_type=jnp.float32,
    )


def start_table(rank, width):
    freq = np.arange(1, rank + 1, dtype=np.int64)[:, None]
    cell = 2 * np.arange(width, dtype=np.int64)[None, :] + 1
    table = np.cos((freq * cell % (4 * width)) * (math.pi / (2 * width))).astype(np.float32)
    high = table.astype(ml_dtypes.bfloat16)
    low = (table - high.astype(np.float32)).astype(ml_dtypes.bfloat16)
    return np.concatenate([high, low], axis=0)


def split(value):
    high = value.astype(jnp.bfloat16)
    return high, (value - high.astype(jnp.float32)).astype(jnp.bfloat16)


def thirds(value):
    first, rest = value.astype(jnp.bfloat16), value
    rest = rest - first.astype(jnp.float32)
    second = rest.astype(jnp.bfloat16)
    return first, second, (rest - second.astype(jnp.float32)).astype(jnp.bfloat16)


def dot_pieces(value, pieces):
    rows = value.shape[0]
    parts = thirds(value)
    total = None
    for index in (2, 1, 0):
        both = dot(jnp.concatenate(parts[: 3 - index], axis=0), pieces[index], (1, 0), None)
        for part in reversed(range(3 - index)):
            term = both[rows * part : rows * (part + 1)]
            total = term if total is None else total + term
    return total


def inverse_factor(image, coeff):
    rank = coeff.shape[0]
    wide = dot(image, jnp.concatenate([coeff, coeff], axis=0), (1, 1))
    row = lax.broadcasted_iota(jnp.int32, wide.shape, 0)
    lane = lax.broadcasted_iota(jnp.int32, wide.shape, 1)
    diag = lane == row + rank
    trace = jnp.sum(jnp.where(diag, wide, 0.0))
    shift = 1e-05 * trace / rank + 1e-06
    work = jnp.where(
        lane >= rank,
        wide + jnp.where(diag, shift, 0.0),
        jnp.where(lane == row, 1.0, 0.0),
    )
    count = rank // SUB
    blocks = [work[SUB * b : SUB * (b + 1)] for b in range(count)]
    below = lax.broadcasted_iota(jnp.int32, (SUB, 2 * rank), 0)
    for p in range(count):
        cols = [
            {
                b: jnp.broadcast_to(
                    blocks[b][:, rank + SUB * p + t : rank + SUB * p + t + 1], (SUB, 2 * rank)
                )
                for b in range(p, count)
            }
            for t in range(SUB)
        ]
        for t in range(SUB):
            inverse = 1.0 / cols[t][p][t : t + 1]
            factor = {b: cols[t][b] * inverse for b in range(p, count)}
            factor[p] = jnp.where(below > t, factor[p], 0.0)
            for u in range(t + 1, SUB):
                top = cols[u][p][t : t + 1]
                for b in range(p, count):
                    cols[u][b] = cols[u][b] - factor[b] * top
            lead = blocks[p][t : t + 1]
            for b in range(p, count):
                blocks[b] = blocks[b] - factor[b] * lead
    work = jnp.concatenate(blocks, axis=0)
    pivots = jnp.sum(jnp.where(diag, work, 0.0), axis=1, keepdims=True)
    return (work / jnp.sqrt(pivots))[:, :rank]


def sweeps(seen, gram_left, gram_right, to_right, to_left):
    for _ in range(2):
        coeff = to_right(seen)
        image = dot_pieces(coeff, gram_right)
        seen = dot(inverse_factor(image, coeff), image)
        coeff = to_left(seen)
        image = dot_pieces(coeff, gram_left)
        inverse = inverse_factor(image, coeff)
        seen = dot(inverse, image)
    return dot(inverse, coeff), to_right(seen)


def layer_kernel(layers, triples, tl, tr, inner, table, lu, ru, out, xs, ys, kmat, sems):
    rank = tl.shape[0]
    slots = triples.shape[0]
    copies = []
    for slot in range(slots):
        chosen = jnp.maximum(triples[slot], 0)
        place = pl.ds((2 + slot) * rank, rank)
        for side, (src, dst) in enumerate(((lu, xs), (ru, ys))):
            copy = pltpu.make_async_copy(src.at[chosen], dst.at[place], sems.at[side, slot])
            copy.start()
            copies.append(copy)
    for src, dst in ((tl, xs), (tr, ys)):
        high, low = split(src[...])
        dst[pl.ds(0, rank)] = high
        dst[pl.ds(rank, rank)] = low
    shape = (rank, 2 * rank)
    row = lax.broadcasted_iota(jnp.int32, shape, 0)
    lane = lax.broadcasted_iota(jnp.int32, shape, 1)
    pair = jnp.where((lane == row) | (lane == row + rank), 1.0 / layers, 0.0)
    kmat[0, pl.ds(0, rank)] = pair
    kmat[0, pl.ds(rank, rank)] = pair
    for slot in range(slots):
        panel = triples[slot]
        valid = jnp.where(panel >= 0, -1.0, 0.0)
        block = inner[jnp.maximum(panel, 0)].astype(jnp.float32) * valid
        half = slot % 2
        mine = (lane >= rank) if half else (lane < rank)
        kmat[1 + slot // 2, pl.ds(half * rank, rank)] = jnp.where(mine, block, 0.0)
    for copy in copies:
        copy.wait()
    left = xs[...]
    right = ys[...]
    gram_left = thirds(dot(left, left, (1, 1), None))
    gram_right = thirds(dot(right, right, (1, 1), None))
    seen = dot(table[...], left, (1, 1), None)
    seen = seen[:rank] + seen[rank:]
    pairs = kmat.shape[0]

    def to_right(value):
        return jnp.concatenate(
            [dot(value[:, LANES * b : LANES * (b + 1)], kmat[b]) for b in range(pairs)], axis=1
        )

    def to_left(value):
        return jnp.concatenate(
            [dot(value[:, LANES * b : LANES * (b + 1)], kmat[b], (1, 1)) for b in range(pairs)],
            axis=1,
        )

    probe, image = sweeps(seen, gram_left, gram_right, to_right, to_left)
    for index, (coeff, stack) in enumerate(((probe, xs), (image, ys))):
        both = dot(jnp.concatenate(split(coeff), axis=0), stack[...], (1, 0), None)
        out[index] = both[:rank] + both[rank:]


def join_kernel(share, upper, mine, other, table, new_left, new_right):
    rank = mine.shape[1]
    width = mine.shape[2]
    is_upper = upper[0] == 1
    both = 2 * rank
    stacks = []
    for index in range(2):
        a, b = mine[index], other[index]
        value = jnp.concatenate([jnp.where(is_upper, b, a), jnp.where(is_upper, a, b)], axis=0)
        stacks.append(jnp.concatenate(split(value), axis=0))
    left, right = stacks

    def folded(stack):
        gram = dot(stack, stack, (1, 1), None)
        gram = gram[:both] + gram[both:]
        return thirds(gram[:, :both] + gram[:, both:])

    seen = dot(table[...], left, (1, 1), None)
    seen = seen[:rank] + seen[rank:]
    seen = seen[:, :both] + seen[:, both:]
    probe, image = sweeps(seen, folded(left), folded(right), lambda v: v, lambda v: v)
    scale = math.sqrt(width)

    def expand(coeff, stack):
        pieces = jnp.concatenate(split(coeff), axis=0)
        half = jnp.where(is_upper, stack[:, share:], stack[:, :share])
        out = dot(jnp.concatenate([pieces, pieces], axis=1), half, (1, 0), None)
        return out[:rank] + out[rank:]

    new_left[0, 0] = expand(probe, left) * scale
    new_right[0, 0] = expand(image, right) / scale


def gathered(left_u, left_v, rank_left, right_u, right_v, rank_right):
    row_u, row_v, row_rank = (
        lax.all_gather(x, "cols", axis=1, tiled=True)[0, :, 0] for x in (left_u, left_v, rank_left)
    )
    col_u, col_v, col_rank = (
        lax.all_gather(x, "rows", axis=1, tiled=True)[0, :, 0]
        for x in (right_u, right_v, rank_right)
    )
    rank = row_v.shape[1]
    index = jnp.arange(rank)
    inner = jnp.einsum("kan,kbn->kab", row_v, col_v, preferred_element_type=jnp.float32)
    keep = (index[None, :, None] < row_rank[:, None, None]) & (
        index[None, None, :] < col_rank[:, None, None]
    )
    inner = jnp.where(keep, inner, 0.0).astype(jnp.bfloat16)
    return row_u, col_u, jnp.concatenate([inner, inner], axis=2)


MESH = pl.DeviceIdType.MESH


def panels_kernel(n_r, n_c, lu, lv, ru, rv, lu_all, ru_all, inner_all, lv_in, rv_mid, rv_in, own,
                  local_sem, mid_send, mid_recv, rv_send, rv_recv, lv_send, lv_recv, lu_send, lu_recv,
                  ru_send, ru_recv, right_send, left_send, in_send, in_recv):
    r = lax.axis_index("rows")
    c = lax.axis_index("cols")
    d = lax.axis_index("depth")
    total = n_r * n_c
    flat = r * n_c + c
    panel = c * n_r + r
    rank = lv.shape[1]

    def remote(src, dst, send, recv, row, col):
        return pltpu.make_async_remote_copy(
            src_ref=src, dst_ref=dst, send_sem=send, recv_sem=recv,
            device_id=(row, col, d), device_id_type=MESH)

    def arrived(dst, send, recv):
        remote(dst, dst, send, recv, lax.rem(r + 1, n_r), c).wait_recv()

    barrier = pltpu.get_barrier_semaphore()
    for t in range(1, total):
        to = lax.rem(flat + t, total)
        pl.semaphore_signal(barrier, inc=1, device_id=(to // n_c, lax.rem(to, n_c), d),
                            device_id_type=MESH)
    pl.semaphore_wait(barrier, total - 1)

    def mid_copy(t):
        to = lax.rem(r + t, n_r)
        return remote(rv.at[to], rv_mid.at[r], mid_send.at[t], mid_recv.at[r], to, c)

    def rv_copy(t):
        to = lax.rem(c + t, n_c)
        return remote(rv_mid.at[to], rv_in.at[c], rv_send.at[t], rv_recv.at[c], r, to)

    def lv_copy(t):
        to = lax.rem(r + t, n_r)
        return remote(lv.at[to], lv_in.at[r], lv_send.at[t], lv_recv.at[r], to, c)

    def lu_copy(side):
        return [
            remote(lu.at[q], lu_all.at[c, q], lu_send.at[side, q], lu_recv.at[c, q], r,
                   c + (1 if side else -1))
            for q in range(lu.shape[0])
        ]

    def ru_copy(t):
        return remote(ru, ru_all.at[r], ru_send.at[t], ru_recv.at[r], lax.rem(r + t, n_r), c)

    @pl.when(c + 1 < n_c)
    def _():
        for copy in lu_copy(1):
            copy.start()

    @pl.when(c > 0)
    def _():
        for copy in lu_copy(0):
            copy.start()

    for t in range(1, n_r):
        mid_copy(t).start()
    own_mid = pltpu.make_async_copy(rv.at[r], rv_mid.at[r], local_sem.at[5])
    own_mid.start()
    own_rv = pltpu.make_async_copy(rv_mid.at[c], rv_in.at[c], local_sem.at[0])
    own_lv = pltpu.make_async_copy(lv.at[r], lv_in.at[r], local_sem.at[1])
    own_lu = pltpu.make_async_copy(lu, lu_all.at[c], local_sem.at[2])
    own_ru = pltpu.make_async_copy(ru, ru_all.at[r], local_sem.at[3])
    for t in range(1, n_r):
        lv_copy(t).start()

    for t in range(1, n_r):
        ru_copy(t).start()

    own_lv.start()
    own_lu.start()
    own_ru.start()
    own_mid.wait()
    for t in range(1, n_r):
        source = lax.rem(r + t, n_r)
        arrived(rv_mid.at[source], mid_send.at[t], mid_recv.at[source])
    for t in range(1, n_c):
        rv_copy(t).start()
    own_rv.start()

    def pass_right(t, q):
        s = c - t
        return remote(lu_all.at[s, q], lu_all.at[s, q], right_send.at[t, q], lu_recv.at[s, q], r, c + 1)

    def pass_left(t, q):
        s = c + t
        return remote(lu_all.at[s, q], lu_all.at[s, q], left_send.at[t, q], lu_recv.at[s, q], r, c - 1)

    def relay_one(t, q):
        @pl.when(c - t >= 0)
        def _():
            arrived(lu_all.at[c - t, q], right_send.at[t, q], lu_recv.at[c - t, q])

            @pl.when(c + 1 < n_c)
            def _():
                pass_right(t, q).start()

        @pl.when(c + t < n_c)
        def _():
            arrived(lu_all.at[c + t, q], left_send.at[t, q], lu_recv.at[c + t, q])

            @pl.when(c > 0)
            def _():
                pass_left(t, q).start()

    def relay(t):
        for q in range(lu.shape[0]):
            relay_one(t, q)

    for t in range(1, n_c - 1):
        relay(t)
    for t in range(1, n_c):
        source = lax.rem(c + t, n_c)
        arrived(rv_in.at[source], rv_send.at[t], rv_recv.at[source])
    own_rv.wait()
    own_lv.wait()
    for t in range(1, n_r):
        source = lax.rem(r + t, n_r)
        arrived(lv_in.at[source], lv_send.at[t], lv_recv.at[source])
    lefts = lv_in[...].reshape(n_r * rank, lv_in.shape[2])
    for j in range(n_c):
        right = rv_in[j]
        both = jnp.concatenate([right, right], axis=0)
        inner = dot(lefts, both, (1, 1), None).astype(jnp.bfloat16)
        own[j] = inner.reshape(n_r, rank, 2 * rank)

    def in_copy(t):
        to = lax.rem(flat + t, total)
        row = to // n_c
        col = lax.rem(to, n_c)
        return remote(own.at[col, row], inner_all.at[panel], in_send.at[t], in_recv.at[panel], row, col)

    for t in range(1, total):
        in_copy(t).start()
    own_inner = pltpu.make_async_copy(own.at[c, r], inner_all.at[panel], local_sem.at[4])
    own_inner.start()
    relay(n_c - 1)
    for t in range(1, n_r):
        source = lax.rem(r + t, n_r)
        arrived(ru_all.at[source], ru_send.at[t], ru_recv.at[source])
    for t in range(1, total):
        source = lax.rem(panel + t, total)
        arrived(inner_all.at[source], in_send.at[t], in_recv.at[source])
    own_inner.wait()
    own_lu.wait()
    own_ru.wait()
    for t in range(1, n_c):
        rv_copy(t).wait_send()
    for t in range(1, n_r):
        mid_copy(t).wait_send()
        lv_copy(t).wait_send()
        ru_copy(t).wait_send()

    @pl.when(c + 1 < n_c)
    def _():
        for copy in lu_copy(1):
            copy.wait_send()

    @pl.when(c > 0)
    def _():
        for copy in lu_copy(0):
            copy.wait_send()

    for t in range(1, n_c):
        @pl.when(jnp.logical_and(c - t >= 0, c + 1 < n_c))
        def _():
            for q in range(lu.shape[0]):
                pass_right(t, q).wait_send()

        @pl.when(jnp.logical_and(c + t < n_c, c > 0))
        def _():
            for q in range(lu.shape[0]):
                pass_left(t, q).wait_send()
    for t in range(1, total):
        in_copy(t).wait_send()


def exchanged(left_u, left_v, rank_left, right_u, right_v, rank_right):
    n_r = lax.axis_size("rows")
    n_c = lax.axis_size("cols")
    lu, lv, rl = (x[0, :, 0] for x in (left_u, left_v, rank_left))
    ru, rv, rr = (x[0, :, 0] for x in (right_u, right_v, rank_right))
    rank, width = lu.shape[1:]
    index = jnp.arange(rank)
    lv = jnp.where((index[None, :] < rl[:, None])[:, :, None], lv, 0)
    rv = jnp.where((index[None, :] < rr[:, None])[:, :, None], rv, 0)
    hbm = pl.BlockSpec(memory_space=pl.ANY)
    total = n_r * n_c
    per = lu.shape[0]
    bf16 = jnp.bfloat16
    dma = pltpu.SemaphoreType.DMA
    lu_all, ru_all, inner = pl.pallas_call(
        lambda *refs: panels_kernel(n_r, n_c, *refs),
        out_shape=(
            jax.ShapeDtypeStruct((n_c,) + lu.shape, bf16),
            jax.ShapeDtypeStruct((n_r,) + ru.shape, bf16),
            jax.ShapeDtypeStruct((total, rank, 2 * rank), bf16),
        ),
        in_specs=[hbm] * 4,
        out_specs=(hbm, hbm, hbm),
        scratch_shapes=[
            pltpu.VMEM((n_r, rank, width), bf16),
            pltpu.VMEM((n_r, rank, width), bf16),
            pltpu.VMEM((n_c, rank, width), bf16),
            pltpu.VMEM((n_c, n_r, rank, 2 * rank), bf16),
            dma((6,)), dma((n_r,)), dma((n_r,)),
            dma((n_c,)), dma((n_c,)), dma((n_r,)), dma((n_r,)),
            dma((2, per)), dma((n_c, per)), dma((n_r,)), dma((n_r,)),
            dma((n_c, per)), dma((n_c, per)), dma((total,)), dma((total,)),
        ],
        compiler_params=pltpu.CompilerParams(
            collective_id=0, has_side_effects=True, vmem_limit_bytes=56 * 2**20),
        name="panels",
    )(lu, lv, ru, rv)
    return (lu_all.reshape(total, rank, width), ru_all.reshape(total, rank, width), inner)


def shards(tile_left, tile_right, left_u, left_v, rank_left, right_u, right_v, rank_right, triples):
    layers = lax.axis_size("depth")
    rank, width = tile_left.shape[2:]
    slots = triples.shape[3]
    share = width // layers
    sizes = {lax.axis_size("rows"), lax.axis_size("cols"), left_u.shape[1], right_u.shape[1]}
    bring = exchanged if len(sizes) == 1 else gathered
    row_u, col_u, inner = bring(left_u, left_v, rank_left, right_u, right_v, rank_right)
    table = jnp.asarray(start_table(rank, width))
    smem = pl.BlockSpec(memory_space=pltpu.SMEM)
    vmem = pl.BlockSpec(memory_space=pltpu.VMEM)
    hbm = pl.BlockSpec(memory_space=pl.ANY)
    stack = (2 + slots) * rank
    params = pltpu.CompilerParams(vmem_limit_bytes=56 * 2**20)
    factors = pl.pallas_call(
        lambda *refs: layer_kernel(layers, *refs),
        out_shape=jax.ShapeDtypeStruct((2, rank, width), jnp.float32),
        in_specs=[smem, vmem, vmem, vmem, vmem, hbm, hbm],
        out_specs=vmem,
        scratch_shapes=[
            pltpu.VMEM((stack, width), jnp.bfloat16),
            pltpu.VMEM((stack, width), jnp.bfloat16),
            pltpu.VMEM((stack // LANES, LANES, LANES), jnp.float32),
            pltpu.SemaphoreType.DMA((2, slots)),
        ],
        compiler_params=params,
        name="layer",
    )(triples[0, 0, 0], tile_left[0, 0], tile_right[0, 0], inner, table, row_u, col_u)
    other = lax.ppermute(factors, "depth", [(d, d ^ 1) for d in range(layers)])
    upper = lax.axis_index("depth").astype(jnp.int32).reshape(1)
    out = jax.ShapeDtypeStruct((1, 1, rank, share), jnp.float32)
    return pl.pallas_call(
        lambda *refs: join_kernel(share, *refs),
        out_shape=(out, out),
        in_specs=[smem, vmem, vmem, vmem],
        out_specs=(vmem, vmem),
        compiler_params=params,
        name="join",
    )(upper, factors, other, table)


def solution(mesh):
    in_specs = (
        P("rows", "cols", None, None),
        P("rows", "cols", None, None),
        P("depth", "cols", "rows", None, None),
        P("depth", "cols", "rows", None, None),
        P("depth", "cols", "rows"),
        P("depth", "rows", "cols", None, None),
        P("depth", "rows", "cols", None, None),
        P("depth", "rows", "cols"),
        P("rows", "cols", "depth", None),
    )
    out_specs = (P("rows", "cols", None, "depth"), P("rows", "cols", None, "depth"))
    return jax.shard_map(shards, mesh=mesh, in_specs=in_specs, out_specs=out_specs, check_vma=False)
```
